32 devices in a mesh: tm: 8 (over z, core), lat: 4 (over y, x).
Axes of the slice: x: 2, y: 2, z: 4, core: 2. Of those that a mesh axis runs over, the one named last changes fastest.
Arguments:
- control: float32 [8, 128, 4096], P('tm', 'lat'), may hold values from -6 to 6
- scales: float32 [8, 128, 4096], P('tm', 'lat'), may hold values from 0.25 to 2
- courant: float32 [8, 128, 4096], P('tm', 'lat'), may hold values from -0.7 to 0.7
- diffusion: float32 [8, 128, 4096], P('tm', 'lat'), may hold values from 0.01 to 0.075
- pacing: float32 [8, 16], P('tm'), may hold values from 0.5 to 1
Outputs:
- defect: float32 [8, 128, 4096], P('tm', 'lat')
- final_state: float32 [8, 128, 4096], P('tm', 'lat')
The draws below stay inside these ranges and needn't reach their ends.
All inputs are finite; a program needn't handle non-finite values.
Results may differ from the reference program's by a relative error of at most 0.00002.
Values sent between devices are 32-bit elements; how exact they have to be, the bound alone decides.
No kernel may reach another device: no remote copies, remote signals or barrier semaphores. Data moves between devices by JAX's collectives and lax.ppermute only.
A program may use at most 64 MiB of HBM per device.

```python
import math
import jax
import jax.numpy as jnp

NLON = 4096
STEPS = 16
WINDOWS = 8
NLAT = 128


def levels(rng, extent, pieces, smallest, high):
    def one(dim, blocks):
        draws = jax.random.uniform(jax.random.fold_in(jax.random.fold_in(rng, 6), dim), (blocks,), jnp.float32, smallest / len(pieces), high / len(pieces))
        return jnp.repeat(jnp.exp(draws), extent[dim] // blocks).reshape((-1,) + (1,) * (len(extent) - dim - 1))

    loudness = one(*pieces[0])
    for cut in pieces[1:]:
        loudness = loudness * one(*cut)
    return loudness


def scatter_about(stream_key, shape, scale, limit, shards=(), dtype=jnp.bfloat16):
    gain = levels(stream_key, shape, shards, -0.22, 0.18) if shards else 1.0
    entries = jax.random.normal(stream_key, shape, jnp.float32) * scale * gain
    return jnp.minimum(jnp.maximum(entries, -limit), limit).astype(dtype)


def setup_inputs(seed: int = 0) -> dict:
    keys = jax.random.split(jax.random.key(seed), 6)
    control = scatter_about(keys[0], (WINDOWS, NLAT, NLON), 1.0, 6.0, ((0, 8), (1, 4)), jnp.float32)
    scales = jnp.clip(jnp.exp(math.log(2.0) - 2.0794415 * jax.random.uniform(keys[1], (WINDOWS, NLAT, NLON), jnp.float32) ** levels(keys[1], (WINDOWS, NLAT, NLON), ((0, 8), (1, 4)), -0.2, 0.2)), 0.25, 2.0)
    courant = jnp.clip(jax.random.uniform(keys[2], (WINDOWS, NLAT, NLON), jnp.float32, -0.7, 0.7) * levels(keys[2], (WINDOWS, NLAT, NLON), ((0, 8), (1, 4)), -0.4, 0.0), -0.7, 0.7)
    diffusion = jnp.clip(jnp.exp(math.log(0.075) - 2.014903 * jax.random.uniform(keys[3], (WINDOWS, NLAT, NLON), jnp.float32) ** levels(keys[3], (WINDOWS, NLAT, NLON), ((0, 8), (1, 4)), -0.2, 0.2)), 0.01, 0.075)
    pacing = jnp.clip(jnp.exp(math.log(1.0) - 0.6931472 * jax.random.uniform(keys[4], (WINDOWS, STEPS), jnp.float32) ** levels(keys[4], (WINDOWS, STEPS), ((0, 8),), -0.2, 0.2)), 0.5, 1.0)
    return {"control": control, "scales": scales, "courant": courant, "diffusion": diffusion, "pacing": pacing}


def advance(extended, courant, diffusion_now):
    centre = extended[:, 1:-1]
    southern = extended[:, :-2]
    northern = extended[:, 2:]
    eastern = jnp.roll(centre, -1, axis=2)
    western = jnp.roll(centre, 1, axis=2)
    upwind_pos = jnp.maximum(courant, 0.0)
    upwind_neg = jnp.minimum(courant, 0.0)
    return (centre - upwind_pos * (centre - southern) - upwind_neg * (northern - centre)
            + diffusion_now * (northern + southern + eastern + western - 4.0 * centre))


def reference(control, scales, courant, diffusion, pacing):
    start_state = jnp.cumsum(scales * control, axis=0)
    current = start_state
    for turn_index in range(STEPS):
        extended = jnp.pad(current, ((0, 0), (1, 1), (0, 0)))
        current = advance(extended, courant, diffusion * pacing[:, turn_index][:, None, None])
    final_state = current
    previous = jnp.concatenate([jnp.zeros_like(final_state[:1]), final_state[:-1]], axis=0)
    return start_state - previous, final_state
```

```python
import functools

import jax
import jax.numpy as jnp
from jax import lax
from jax.experimental import pallas as pl
from jax.experimental.pallas import tpu as pltpu
from jax.sharding import PartitionSpec as P

LANES = 128
SUBLANES = 8


def up_to(value, multiple):
    return -(-value // multiple) * multiple


def steps_kernel(steps, rows, places, own, other, before, after, courant, diffusion, coef_before,
                 coef_after, pacing, out, even, odd, c_all, d_all):
    halves, tiles = 2, courant.shape[1] // LANES
    half = tiles // halves
    base = SUBLANES
    total = rows + 2 * steps
    core, has_before, has_after = places[0], places[1], places[2]
    here = slice(base + steps, base + steps + rows)
    south = slice(base, base + steps)
    north = slice(base + steps + rows, base + total)
    for t in range(half):
        cols = slice(t * LANES, (t + 1) * LANES)
        for which, source in ((0, own), (1, other)):
            to = 1 + t + half * jnp.where(core == which, 0, 1)
            even[to, here, :] = source[:, cols]
            even[to, south, :] = jnp.where(has_before > 0, before[which, :, cols], 0.0)
            even[to, north, :] = jnp.where(has_after > 0, after[which, :, cols], 0.0)
    for t in range(tiles):
        cols = slice(t * LANES, (t + 1) * LANES)
        for which, source, scratch in ((0, courant, c_all), (1, diffusion, d_all)):
            scratch[t, here, :] = source[:, cols]
            scratch[t, south, :] = jnp.where(has_before > 0, coef_before[which, :, cols], 0.0)
            scratch[t, north, :] = jnp.where(has_after > 0, coef_after[which, :, cols], 0.0)
    for step in range(1, steps + 1):
        old, new = (even, odd) if step % 2 else (odd, even)
        count = up_to(total - 2 * step, SUBLANES)
        first = base + step
        pace = pacing[0, step - 1]
        old[0, :, :] = old[tiles, :, :]
        old[tiles + 1, :, :] = old[1, :, :]
        lane = lax.broadcasted_iota(jnp.int32, (count, LANES), 1)
        window = slice(first, first + count)
        for t in range(1, tiles + 1):
            x = old[t, window, :]
            east = pltpu.roll(jnp.where(lane == 0, old[t + 1, window, :], x), LANES - 1, 1)
            west = pltpu.roll(jnp.where(lane == LANES - 1, old[t - 1, window, :], x), 1, 1)
            ahead = old[t, first + 1 : first + 1 + count, :] - x
            behind = x - old[t, first - 1 : first - 1 + count, :]
            c = c_all[t - 1, window, :]
            d = d_all[t - 1, window, :]
            spread = ((east - x) + (west - x)) + (ahead - behind)
            new[t, window, :] = x + (d * pace) * spread - c * jnp.where(c > 0, behind, ahead)
    last = odd if steps % 2 else even
    for t in range(tiles):
        out[:, t * LANES : (t + 1) * LANES] = last[t + 1, here, :]


def run_steps(steps, places, own, other, before, after, courant, diffusion, coef_before, coef_after, pacing):
    rows, columns = courant.shape
    tiles = columns // LANES
    depth = SUBLANES + rows + 2 * steps + 2 * SUBLANES
    smem = pl.BlockSpec(memory_space=pltpu.SMEM)
    vmem = pl.BlockSpec(memory_space=pltpu.VMEM)
    return pl.pallas_call(
        functools.partial(steps_kernel, steps, rows),
        out_shape=jax.ShapeDtypeStruct((rows, columns), jnp.float32),
        in_specs=[smem] + [vmem] * 8 + [smem],
        out_specs=vmem,
        scratch_shapes=[pltpu.VMEM((tiles + 2, depth, LANES), jnp.float32)] * 2
        + [pltpu.VMEM((tiles, depth, LANES), jnp.float32)] * 2,
        compiler_params=pltpu.CompilerParams(vmem_limit_bytes=40 * 2**20),
    )(places, own, other, before, after, courant, diffusion, coef_before, coef_after, pacing)


def on_device(control, scales, courant, diffusion, pacing):
    control, scales, courant, diffusion = (v[0] for v in (control, scales, courant, diffusion))
    steps = pacing.shape[1]
    rows, columns = control.shape
    half = columns // 2
    windows, bands = lax.axis_size("tm"), lax.axis_size("lat")
    window, band = lax.axis_index("tm"), lax.axis_index("lat")
    core, chip = window % 2, window // 2
    is_first = core == 0
    onward = [(i, (i + 1) % bands) for i in range(bands)]
    backward = [(j, i) for i, j in onward]
    partner = [(i, i ^ 1) for i in range(windows)]

    increment = scales * control
    left, right = increment[:, :half], increment[:, half:]
    own = jnp.where(is_first, left, right)
    other = jnp.where(is_first, right, left)

    coefficients = jnp.stack([courant, diffusion])
    coef_before = lax.ppermute(coefficients[:, rows - steps :], "lat", onward)
    coef_after = lax.ppermute(coefficients[:, :steps], "lat", backward)

    pair = own + lax.ppermute(other, "tm", partner)
    total, before = pair, jnp.zeros_like(pair)
    distance = 1
    while 2 * distance < windows:
        swap = [(i, i ^ (2 * distance)) for i in range(windows)]
        arrived = lax.ppermute(total, "tm", swap)
        before = before + jnp.where((chip // distance) % 2 == 1, arrived, 0.0)
        total = total + arrived
        distance *= 2
    through_first = before + own
    arrived = lax.ppermute(jnp.where(is_first, through_first, before), "tm", partner)
    start_own = jnp.where(is_first, through_first, before + pair)
    start_other = arrived + other

    start_before = lax.ppermute(jnp.stack([start_own[rows - steps :], start_other[rows - steps :]]), "lat", onward)
    start_after = lax.ppermute(jnp.stack([start_own[:steps], start_other[:steps]]), "lat", backward)
    places = jnp.stack([core, band, bands - 1 - band]).astype(jnp.int32)
    final = run_steps(steps, places, start_own, start_other, start_before, start_after, courant, diffusion,
                      coef_before, coef_after, pacing)
    previous = lax.ppermute(final, "tm", [(i, i + 1) for i in range(windows - 1)])
    start = jnp.where(is_first, jnp.concatenate([start_own, start_other], axis=1),
                      jnp.concatenate([start_other, start_own], axis=1))
    return (start - previous)[None], final[None]


def solution(mesh):
    whole = P("tm", "lat", None)
    return jax.shard_map(
        on_device,
        mesh=mesh,
        in_specs=(whole, whole, whole, whole, P("tm", None)),
        out_specs=(whole, whole),
        check_vma=False,
    )
```

```python
import functools

import jax
import jax.numpy as jnp
from jax import lax
from jax.experimental import pallas as pl
from jax.experimental.pallas import tpu as pltpu
from jax.sharding import PartitionSpec as P

LANES = 128
VMEM = pl.BlockSpec(memory_space=pltpu.VMEM)


def call(kernel, out_shapes, args, aliases=None, work=0):
    return pl.pallas_call(
        kernel,
        out_shape=tuple(pltpu.VMEM(shape, jnp.float32) for shape in out_shapes),
        in_specs=[VMEM] * len(args),
        out_specs=(VMEM,) * len(out_shapes),
        input_output_aliases=aliases or {},
        cost_estimate=pl.CostEstimate(flops=work, bytes_accessed=0, transcendentals=0),
        compiler_params=pltpu.CompilerParams(vmem_limit_bytes=4 * 2**20),
    )(*(pltpu.with_memory_space_constraint(v, pltpu.VMEM) for v in args))


def has_band_before():
    return lax.axis_index("lat") > 0


def has_band_after():
    return lax.axis_index("lat") < lax.axis_size("lat") - 1


def columns_of(tile):
    return slice(tile * LANES, (tile + 1) * LANES)


def advance_rows(steps, rows_of, old_and_new, c_all, d_all, paces):
    tiles = c_all.shape[0]
    for step in range(1, steps + 1):
        first, stop = rows_of(step)
        if first >= stop:
            continue
        old, new = old_and_new if step % 2 else old_and_new[::-1]
        pace = paces[step - 1 : step, :]
        lane = lax.broadcasted_iota(jnp.int32, (stop - first, LANES), 1)
        for t in range(tiles):
            x = old[t, first:stop, :]
            east = pltpu.roll(jnp.where(lane == 0, old[(t + 1) % tiles, first:stop, :], x), LANES - 1, 1)
            west = pltpu.roll(jnp.where(lane == LANES - 1, old[(t - 1) % tiles, first:stop, :], x), 1, 1)
            ahead = old[t, first + 1 : stop + 1, :] - x
            behind = x - old[t, first - 1 : stop - 1, :]
            c = c_all[t, first:stop, :]
            d = d_all[t, first:stop, :]
            spread = ((east - x) + (west - x)) + (ahead - behind)
            new[t, first:stop, :] = x + (d * pace) * spread - c * jnp.where(c > 0, behind, ahead)


def coefficients_kernel(steps, courant, diffusion, *rest):
    outer, (c_all, d_all) = rest[:4], rest[4:]
    rows, tiles = courant.shape[0], c_all.shape[0]
    has_before, has_after = has_band_before(), has_band_after()
    for t in range(tiles):
        for field, south, north, whole in ((courant, *outer[:2], c_all), (diffusion, *outer[2:], d_all)):
            whole[t, steps : steps + rows, :] = field[:, columns_of(t)]
            whole[t, :steps, :] = jnp.where(has_before, south[:, columns_of(t)], 0.0)
            whole[t, steps + rows :, :] = jnp.where(has_after, north[:, columns_of(t)], 0.0)


def place_halves(own, other, rows, whole):
    half = whole.shape[0] // 2
    for t in range(half):
        for which, source in ((0, own), (1, other)):
            to = t + half * jnp.where(lax.axis_index("tm") % 2 == which, 0, 1)
            whole[to, rows, :] = source(columns_of(t))


def inner_kernel(steps, paces, own, other, c_all, d_all, even, odd):
    rows = own.shape[0]
    place_halves(lambda cols: own[:, cols], lambda cols: other[:, cols], slice(steps, steps + rows), even)
    advance_rows(steps, lambda n: (steps + n, steps + rows - n), (even, odd), c_all, d_all, paces)


def south_kernel(steps, paces, halo, c_all, d_all, even_in, odd_in, even, odd, outer, final):
    del even_in, odd_in
    exists = has_band_before()
    place_halves(lambda cols: jnp.where(exists, halo[:steps, cols], 0.0),
                 lambda cols: jnp.where(exists, halo[steps:, cols], 0.0), slice(0, steps), even)
    advance_rows(steps, lambda n: (n, steps + n), (even, odd), c_all, d_all, paces)
    last = odd if steps % 2 else even
    for t in range(last.shape[0]):
        outer[:, columns_of(t)] = last[t, steps : 2 * steps, :]
        final[:steps, columns_of(t)] = last[t, steps : 2 * steps, :]


def north_kernel(steps, paces, halo, c_all, d_all, even_in, odd_in, final_in, even, odd, outer, final):
    del even_in, odd_in, final_in
    exists = has_band_after()
    rows = final.shape[0]
    place_halves(lambda cols: jnp.where(exists, halo[:steps, cols], 0.0),
                 lambda cols: jnp.where(exists, halo[steps:, cols], 0.0), slice(steps + rows, 2 * steps + rows), even)
    advance_rows(steps, lambda n: (steps + rows - n, 2 * steps + rows - n), (even, odd), c_all, d_all, paces)
    last = odd if steps % 2 else even
    for t in range(last.shape[0]):
        outer[:, columns_of(t)] = last[t, rows : steps + rows, :]
        final[steps:, columns_of(t)] = last[t, rows : steps + rows, :]


def on_device(control, scales, courant, diffusion, pacing):
    control, scales, courant, diffusion = (v[0] for v in (control, scales, courant, diffusion))
    steps = pacing.shape[1]
    rows, columns = control.shape
    half, tiles = columns // 2, columns // LANES
    windows, bands = lax.axis_size("tm"), lax.axis_size("lat")
    window = lax.axis_index("tm")
    is_first, chip = window % 2 == 0, window // 2
    onward = [(i, (i + 1) % bands) for i in range(bands)]
    backward = [(j, i) for i, j in onward]
    partner = [(i, i ^ 1) for i in range(windows)]
    following = [(i, i + 1) for i in range(windows - 1)]
    paces = jnp.broadcast_to(pacing.reshape(steps, 1), (steps, LANES))

    increment = scales * control
    left, right = increment[:, :half], increment[:, half:]
    own = jnp.where(is_first, left, right)
    other = jnp.where(is_first, right, left)

    outer = [
        lax.ppermute(part, "lat", way)
        for v in (courant, diffusion)
        for part, way in ((v[rows - steps :], onward), (v[:steps], backward))
    ]

    pair = own + lax.ppermute(other, "tm", partner)
    total, before = pair, jnp.zeros_like(pair)
    distance = 1
    while 2 * distance < windows:
        swap = [(i, i ^ (2 * distance)) for i in range(windows)]
        arrived = lax.ppermute(total, "tm", swap)
        before = before + jnp.where((chip // distance) % 2 == 1, arrived, 0.0)
        total = total + arrived
        distance *= 2
    before, outer = lax.optimization_barrier((before, outer))
    through_first = before + own
    arrived = lax.ppermute(jnp.where(is_first, through_first, before), "tm", partner)
    start_own = jnp.where(is_first, through_first, before + pair)
    start_other = arrived + other

    south = lax.ppermute(jnp.concatenate([start_own[rows - steps :], start_other[rows - steps :]]), "lat", onward)
    north = lax.ppermute(jnp.concatenate([start_own[:steps], start_other[:steps]]), "lat", backward)

    field = (tiles, rows + 2 * steps, LANES)
    part, band_shape = (steps, columns), (rows, columns)
    c_all, d_all = call(functools.partial(coefficients_kernel, steps), [field] * 2,
                        (courant, diffusion, *outer))
    work = 16 * steps * steps * columns
    even, odd = call(functools.partial(inner_kernel, steps), [field] * 2,
                     (paces, start_own, start_other, c_all, d_all), work=work)
    even, odd, final_south, final = call(
        functools.partial(south_kernel, steps), [field, field, part, band_shape],
        (paces, south, c_all, d_all, even, odd), {4: 0, 5: 1}, work=work)
    previous_south = lax.ppermute(final_south, "tm", following)
    _, _, final_north, final = call(
        functools.partial(north_kernel, steps), [field, field, part, band_shape],
        (paces, north, c_all, d_all, even, odd, final), {4: 0, 5: 1, 6: 3}, work=work)
    previous_north = lax.ppermute(final_north, "tm", following)
    start = jnp.where(is_first, jnp.concatenate([start_own, start_other], axis=1),
                      jnp.concatenate([start_other, start_own], axis=1))
    return (start - jnp.concatenate([previous_south, previous_north]))[None], final[None]


def solution(mesh):
    whole = P("tm", "lat", None)
    return jax.shard_map(
        on_device,
        mesh=mesh,
        in_specs=(whole, whole, whole, whole, P("tm", None)),
        out_specs=(whole, whole),
        check_vma=False,
    )
```

```python
import functools

import jax
import jax.numpy as jnp
from jax import lax
from jax.experimental import pallas as pl
from jax.experimental.pallas import tpu as pltpu
from jax.sharding import PartitionSpec as P

LANES = 128
MOVED = 64 * 2**20
VMEM = pl.BlockSpec(memory_space=pltpu.VMEM)


def call(kernel, out_shapes, args, aliases=None, work=0, moved=0):
    return pl.pallas_call(
        kernel,
        out_shape=tuple(pltpu.VMEM(shape, jnp.float32) for shape in out_shapes),
        in_specs=[VMEM] * len(args),
        out_specs=(VMEM,) * len(out_shapes),
        input_output_aliases=aliases or {},
        cost_estimate=pl.CostEstimate(flops=work, bytes_accessed=moved, transcendentals=0),
        compiler_params=pltpu.CompilerParams(vmem_limit_bytes=4 * 2**20),
    )(*(pltpu.with_memory_space_constraint(v, pltpu.VMEM) for v in args))


def has_band_before():
    return lax.axis_index("lat") > 0


def has_band_after():
    return lax.axis_index("lat") < lax.axis_size("lat") - 1


def columns_of(tile):
    return slice(tile * LANES, (tile + 1) * LANES)


def advance_rows(steps, rows_of, old_and_new, c_all, d_all, paces):
    tiles = c_all.shape[0]
    for step in range(1, steps + 1):
        first, stop = rows_of(step)
        if first >= stop:
            continue
        old, new = old_and_new if step % 2 else old_and_new[::-1]
        pace = paces[step - 1 : step, :]
        lane = lax.broadcasted_iota(jnp.int32, (stop - first, LANES), 1)
        for t in range(tiles):
            x = old[t, first:stop, :]
            east = pltpu.roll(jnp.where(lane == 0, old[(t + 1) % tiles, first:stop, :], x), LANES - 1, 1)
            west = pltpu.roll(jnp.where(lane == LANES - 1, old[(t - 1) % tiles, first:stop, :], x), 1, 1)
            ahead = old[t, first + 1 : stop + 1, :] - x
            behind = x - old[t, first - 1 : stop - 1, :]
            c = c_all[t, first:stop, :]
            d = d_all[t, first:stop, :]
            spread = ((east - x) + (west - x)) + (ahead - behind)
            new[t, first:stop, :] = x + (d * pace) * spread - c * jnp.where(c > 0, behind, ahead)


def pack_kernel(steps, courant, diffusion, onward, backward):
    rows = courant.shape[0]
    for at, field in ((0, courant), (steps, diffusion)):
        onward[at : at + steps, :] = field[rows - steps :, :]
        backward[at : at + steps, :] = field[:steps, :]


def coefficients_kernel(steps, courant, diffusion, south, north, c_all, d_all):
    rows, tiles = courant.shape[0], c_all.shape[0]
    has_before, has_after = has_band_before(), has_band_after()
    for t in range(tiles):
        for at, field, whole in ((0, courant, c_all), (steps, diffusion, d_all)):
            whole[t, steps : steps + rows, :] = field[:, columns_of(t)]
            whole[t, :steps, :] = jnp.where(has_before, south[at : at + steps, columns_of(t)], 0.0)
            whole[t, steps + rows :, :] = jnp.where(has_after, north[at : at + steps, columns_of(t)], 0.0)


def place_halves(own, other, rows, whole):
    half = whole.shape[0] // 2
    for t in range(half):
        for which, source in ((0, own), (1, other)):
            to = t + half * jnp.where(lax.axis_index("tm") % 2 == which, 0, 1)
            whole[to, rows, :] = source(columns_of(t))


def inner_kernel(steps, paces, own, other, c_all, d_all, even, odd):
    rows = own.shape[0]
    place_halves(lambda cols: own[:, cols], lambda cols: other[:, cols], slice(steps, steps + rows), even)
    advance_rows(steps, lambda n: (steps + n, steps + rows - n), (even, odd), c_all, d_all, paces)


def south_kernel(steps, paces, halo, c_all, d_all, even_in, odd_in, even, odd, part):
    del even_in, odd_in
    exists = has_band_before()
    place_halves(lambda cols: jnp.where(exists, halo[:steps, cols], 0.0),
                 lambda cols: jnp.where(exists, halo[steps:, cols], 0.0), slice(0, steps), even)
    advance_rows(steps, lambda n: (n, steps + n), (even, odd), c_all, d_all, paces)
    last = odd if steps % 2 else even
    for t in range(last.shape[0]):
        part[:, columns_of(t)] = last[t, steps : 2 * steps, :]


def north_kernel(steps, paces, halo, c_all, d_all, even_in, odd_in, even, odd, part):
    del even_in, odd_in
    exists = has_band_after()
    rows = c_all.shape[1] - 2 * steps
    place_halves(lambda cols: jnp.where(exists, halo[:steps, cols], 0.0),
                 lambda cols: jnp.where(exists, halo[steps:, cols], 0.0), slice(steps + rows, 2 * steps + rows), even)
    advance_rows(steps, lambda n: (steps + rows - n, 2 * steps + rows - n), (even, odd), c_all, d_all, paces)
    last = odd if steps % 2 else even
    for t in range(last.shape[0]):
        part[:, columns_of(t)] = last[t, 2 * steps : steps + rows, :]


def results_kernel(at, previous, own, other, final_part, *refs):
    defect, final, difference, sems = refs[-4:]
    count, half = previous.shape[0], own.shape[1]
    here = pl.ds(at, count)
    kept = pltpu.make_async_copy(final_part, final.at[here], sems.at[0])
    kept.start()
    is_first = lax.axis_index("tm") % 2 == 0
    follows = lax.axis_index("tm") > 0
    for low in range(0, half, LANES):
        a, b = own[at : at + count, low : low + LANES], other[at : at + count, low : low + LANES]
        for cols, start in (
            (slice(low, low + LANES), jnp.where(is_first, a, b)),
            (slice(half + low, half + low + LANES), jnp.where(is_first, b, a)),
        ):
            difference[:, cols] = start - jnp.where(follows, previous[:, cols], 0.0)
    made = pltpu.make_async_copy(difference, defect.at[here], sems.at[1])
    made.start()
    kept.wait()
    made.wait()


def write_results(at, previous, own, other, final_part, earlier):
    shape = (own.shape[0], 2 * own.shape[1])
    hbm = pl.BlockSpec(memory_space=pltpu.HBM)
    return pl.pallas_call(
        functools.partial(results_kernel, at),
        out_shape=(pltpu.HBM(shape, jnp.float32),) * 2,
        in_specs=[VMEM] * 4 + [hbm] * len(earlier),
        out_specs=(hbm, hbm),
        scratch_shapes=[pltpu.VMEM(previous.shape, jnp.float32), pltpu.SemaphoreType.DMA((2,))],
        input_output_aliases={4 + i: i for i in range(len(earlier))},
        compiler_params=pltpu.CompilerParams(vmem_limit_bytes=4 * 2**20),
    )(*(pltpu.with_memory_space_constraint(v, pltpu.VMEM) for v in (previous, own, other, final_part)), *earlier)


def on_device(control, scales, courant, diffusion, pacing):
    control, scales, courant, diffusion = (v[0] for v in (control, scales, courant, diffusion))
    steps = pacing.shape[1]
    rows, columns = control.shape
    half, tiles = columns // 2, columns // LANES
    windows, bands = lax.axis_size("tm"), lax.axis_size("lat")
    window = lax.axis_index("tm")
    is_first, chip = window % 2 == 0, window // 2
    onward = [(i, (i + 1) % bands) for i in range(bands)]
    backward = [(j, i) for i, j in onward]
    partner = [(i, i ^ 1) for i in range(windows)]
    following = [(i, (i + 1) % windows) for i in range(windows)]
    paces = jnp.broadcast_to(pacing.reshape(steps, 1), (steps, LANES))

    increment = scales * control
    left, right = increment[:, :half], increment[:, half:]
    own = jnp.where(is_first, left, right)
    other = jnp.where(is_first, right, left)

    field = (tiles, rows + 2 * steps, LANES)
    to_onward, to_backward = call(functools.partial(pack_kernel, steps), [(2 * steps, columns)] * 2, (courant, diffusion))
    outer = lax.ppermute(to_onward, "lat", onward), lax.ppermute(to_backward, "lat", backward)

    c_all, d_all = call(functools.partial(coefficients_kernel, steps), [field] * 2,
                        (courant, diffusion, *outer), moved=MOVED)

    pair = own + lax.ppermute(other, "tm", partner)
    total, before = pair, jnp.zeros_like(pair)
    distance = 1
    while 2 * distance < windows:
        swap = [(i, i ^ (2 * distance)) for i in range(windows)]
        arrived = lax.ppermute(total, "tm", swap)
        if 4 * distance >= windows:
            arrived, c_all, d_all = lax.optimization_barrier((arrived, c_all, d_all))
        before = before + jnp.where((chip // distance) % 2 == 1, arrived, 0.0)
        total = total + arrived
        distance *= 2
    through_first = before + own
    arrived = lax.ppermute(jnp.where(is_first, through_first, before), "tm", partner)
    start_own = jnp.where(is_first, through_first, before + pair)
    start_other = arrived + other

    south = lax.ppermute(jnp.concatenate([start_own[rows - steps :], start_other[rows - steps :]]), "lat", onward)
    north = lax.ppermute(jnp.concatenate([start_own[:steps], start_other[:steps]]), "lat", backward)

    work = 16 * steps * steps * columns
    even, odd = call(functools.partial(inner_kernel, steps), [field] * 2,
                     (paces, start_own, start_other, c_all, d_all), work=work)
    even, odd, final_south = call(
        functools.partial(south_kernel, steps), [field, field, (steps, columns)],
        (paces, south, c_all, d_all, even, odd), {4: 0, 5: 1}, work=work)
    previous_south = lax.ppermute(final_south, "tm", following)
    _, _, final_north = call(
        functools.partial(north_kernel, steps), [field, field, (rows - steps, columns)],
        (paces, north, c_all, d_all, even, odd), {4: 0, 5: 1}, work=work)
    previous_north = lax.ppermute(final_north, "tm", following)
    results = write_results(0, previous_south, start_own, start_other, final_south, ())
    defect, final = write_results(steps, previous_north, start_own, start_other, final_north, results)
    return defect[None], final[None]


def solution(mesh):
    whole = P("tm", "lat", None)
    return jax.shard_map(
        on_device,
        mesh=mesh,
        in_specs=(whole, whole, whole, whole, P("tm", None)),
        out_specs=(whole, whole),
        check_vma=False,
    )
```

```python
import functools

import jax
import jax.numpy as jnp
from jax import lax
from jax.experimental import pallas as pl
from jax.experimental.pallas import tpu as pltpu
from jax.sharding import PartitionSpec as P

LANES = 128
MOVED = 64 * 2**20
PIECES = 2
VMEM = pl.BlockSpec(memory_space=pltpu.VMEM)


def call(kernel, out_shapes, args, aliases=None, work=0, moved=0):
    return pl.pallas_call(
        kernel,
        out_shape=tuple(pltpu.VMEM(shape, jnp.float32) for shape in out_shapes),
        in_specs=[VMEM] * len(args),
        out_specs=(VMEM,) * len(out_shapes),
        input_output_aliases=aliases or {},
        cost_estimate=pl.CostEstimate(flops=work, bytes_accessed=moved, transcendentals=0),
        compiler_params=pltpu.CompilerParams(vmem_limit_bytes=4 * 2**20),
    )(*(pltpu.with_memory_space_constraint(v, pltpu.VMEM) for v in args))


def has_band_before():
    return lax.axis_index("lat") > 0


def has_band_after():
    return lax.axis_index("lat") < lax.axis_size("lat") - 1


def columns_of(tile):
    return slice(tile * LANES, (tile + 1) * LANES)


def advance_rows(steps, rows_of, old_and_new, c_all, d_all, paces):
    tiles = c_all.shape[0]
    for step in range(1, steps + 1):
        first, stop = rows_of(step)
        if first >= stop:
            continue
        old, new = old_and_new if step % 2 else old_and_new[::-1]
        pace = paces[step - 1 : step, :]
        lane = lax.broadcasted_iota(jnp.int32, (stop - first, LANES), 1)
        for t in ((step + i) % tiles for i in range(tiles)):
            x = old[t, first:stop, :]
            east = pltpu.roll(jnp.where(lane == 0, old[(t + 1) % tiles, first:stop, :], x), LANES - 1, 1)
            west = pltpu.roll(jnp.where(lane == LANES - 1, old[(t - 1) % tiles, first:stop, :], x), 1, 1)
            ahead = old[t, first + 1 : stop + 1, :] - x
            behind = x - old[t, first - 1 : stop - 1, :]
            c = c_all[t, first:stop, :]
            d = d_all[t, first:stop, :]
            spread = ((east - x) + (west - x)) + (ahead - behind)
            new[t, first:stop, :] = x + (d * pace) * spread - c * jnp.where(c > 0, behind, ahead)


def sum_kernel(a, b, total):
    total[:, :] = a[:, :] + b[:, :]


def prefix_kernel(pieces, steps, own, pair, *refs):
    brought, (send, start_own, to_onward, to_backward) = refs[:-4], refs[-4:]
    hops = len(brought) // pieces
    width = own.shape[1] // pieces
    is_first, chip = lax.axis_index("tm") % 2 == 0, lax.axis_index("tm") // 2
    for piece in range(pieces):
        cols = slice(piece * width, (piece + 1) * width)
        before = jnp.where(chip % 2 == 1, brought[piece * hops][:, :], 0.0)
        for hop in range(1, hops):
            before = before + jnp.where(chip == hop + 1, brought[piece * hops + hop][:, :], 0.0)
        through_first = before + own[:, cols]
        send[:, cols] = jnp.where(is_first, through_first, before)
        start_own[:, cols] = jnp.where(is_first, through_first, before + pair[:, cols])
    to_onward[:, :] = start_own[own.shape[0] - steps :, :]
    to_backward[:, :] = start_own[:steps, :]


def halo_kernel(steps, other, arrived, start_other, to_onward, to_backward):
    start_other[:, :] = other[:, :] + arrived[:, :]
    to_onward[:, :] = start_other[other.shape[0] - steps :, :]
    to_backward[:, :] = start_other[:steps, :]


def pack_kernel(steps, courant, diffusion, onward, backward):
    rows = courant.shape[0]
    for at, field in ((0, courant), (steps, diffusion)):
        onward[at : at + steps, :] = field[rows - steps :, :]
        backward[at : at + steps, :] = field[:steps, :]


def inner_coefficients_kernel(steps, courant, diffusion, c_all, d_all):
    rows = courant.shape[0]
    for t in range(c_all.shape[0]):
        c_all[t, steps : steps + rows, :] = courant[:, columns_of(t)]
        d_all[t, steps : steps + rows, :] = diffusion[:, columns_of(t)]


def outer_coefficients_kernel(steps, at, side, c_in, d_in, c_all, d_all):
    del c_in, d_in
    exists = has_band_before() if at == 0 else has_band_after()
    for t in range(c_all.shape[0]):
        for which, whole in enumerate((c_all, d_all)):
            rows = side[which * steps : (which + 1) * steps, columns_of(t)]
            whole[t, at : at + steps, :] = jnp.where(exists, rows, 0.0)


def place_halves(own, other, rows, whole):
    half = whole.shape[0] // 2
    for t in range(half):
        for which, source in ((0, own), (1, other)):
            to = t + half * jnp.where(lax.axis_index("tm") % 2 == which, 0, 1)
            whole[to, rows, :] = source(columns_of(t))


def inner_kernel(steps, paces, own, other, c_all, d_all, even, odd):
    rows = own.shape[0]
    place_halves(lambda cols: own[:, cols], lambda cols: other[:, cols], slice(steps, steps + rows), even)
    advance_rows(steps, lambda n: (steps + n, steps + rows - n), (even, odd), c_all, d_all, paces)


def south_kernel(steps, paces, own, other, c_all, d_all, even_in, odd_in, even, odd, part):
    del even_in, odd_in
    exists = has_band_before()
    place_halves(lambda cols: jnp.where(exists, own[:, cols], 0.0),
                 lambda cols: jnp.where(exists, other[:, cols], 0.0), slice(0, steps), even)
    advance_rows(steps, lambda n: (n, steps + n), (even, odd), c_all, d_all, paces)
    last = odd if steps % 2 else even
    for t in range(last.shape[0]):
        part[:, columns_of(t)] = last[t, steps : 2 * steps, :]


def north_kernel(steps, paces, own, other, c_all, d_all, even_in, odd_in, even, odd, part):
    del even_in, odd_in
    exists = has_band_after()
    rows = c_all.shape[1] - 2 * steps
    place_halves(lambda cols: jnp.where(exists, own[:, cols], 0.0),
                 lambda cols: jnp.where(exists, other[:, cols], 0.0), slice(steps + rows, 2 * steps + rows), even)
    advance_rows(steps, lambda n: (steps + rows - n, 2 * steps + rows - n), (even, odd), c_all, d_all, paces)
    last = odd if steps % 2 else even
    for t in range(last.shape[0]):
        part[:, columns_of(t)] = last[t, 2 * steps : steps + rows, :]


def results_kernel(at, previous, own, other, final_part, *refs):
    defect, final, difference, sems = refs[-4:]
    count, half = previous.shape[0], own.shape[1]
    here = pl.ds(at, count)
    kept = pltpu.make_async_copy(final_part, final.at[here], sems.at[0])
    kept.start()
    is_first = lax.axis_index("tm") % 2 == 0
    follows = lax.axis_index("tm") > 0
    for low in range(0, half, LANES):
        a, b = own[at : at + count, low : low + LANES], other[at : at + count, low : low + LANES]
        for cols, start in (
            (slice(low, low + LANES), jnp.where(is_first, a, b)),
            (slice(half + low, half + low + LANES), jnp.where(is_first, b, a)),
        ):
            difference[:, cols] = start - jnp.where(follows, previous[:, cols], 0.0)
    made = pltpu.make_async_copy(difference, defect.at[here], sems.at[1])
    made.start()
    kept.wait()
    made.wait()


def write_results(at, previous, own, other, final_part, earlier):
    shape = (own.shape[0], 2 * own.shape[1])
    hbm = pl.BlockSpec(memory_space=pltpu.HBM)
    return pl.pallas_call(
        functools.partial(results_kernel, at),
        out_shape=(pltpu.HBM(shape, jnp.float32),) * 2,
        in_specs=[VMEM] * 4 + [hbm] * len(earlier),
        out_specs=(hbm, hbm),
        scratch_shapes=[pltpu.VMEM(previous.shape, jnp.float32), pltpu.SemaphoreType.DMA((2,))],
        input_output_aliases={4 + i: i for i in range(len(earlier))},
        compiler_params=pltpu.CompilerParams(vmem_limit_bytes=4 * 2**20),
    )(*(pltpu.with_memory_space_constraint(v, pltpu.VMEM) for v in (previous, own, other, final_part)), *earlier)


def on_device(control, scales, courant, diffusion, pacing):
    control, scales, courant, diffusion = (v[0] for v in (control, scales, courant, diffusion))
    steps = pacing.shape[1]
    rows, columns = control.shape
    half, tiles = columns // 2, columns // LANES
    windows, bands = lax.axis_size("tm"), lax.axis_size("lat")
    window = lax.axis_index("tm")
    is_first = window % 2 == 0
    onward = [(i, (i + 1) % bands) for i in range(bands)]
    backward = [(j, i) for i, j in onward]
    partner = [(i, i ^ 1) for i in range(windows)]
    following = [(i, (i + 1) % windows) for i in range(windows)]
    paces = jnp.broadcast_to(pacing.reshape(steps, 1), (steps, LANES))

    increment = scales * control
    left, right = increment[:, :half], increment[:, half:]
    own = jnp.where(is_first, left, right)
    other = jnp.where(is_first, right, left)

    field = (tiles, rows + 2 * steps, LANES)
    to_onward, to_backward = call(functools.partial(pack_kernel, steps), [(2 * steps, columns)] * 2, (courant, diffusion))
    coef_south, coef_north = lax.ppermute(to_onward, "lat", onward), lax.ppermute(to_backward, "lat", backward)
    c_all, d_all = call(functools.partial(inner_coefficients_kernel, steps), [field] * 2, (courant, diffusion))
    c_all, d_all = call(functools.partial(outer_coefficients_kernel, steps, 0), [field] * 2,
                        (coef_south, c_all, d_all), {1: 0, 2: 1}, moved=MOVED)

    (pair,) = call(sum_kernel, [own.shape], (own, lax.ppermute(other, "tm", partner)))
    width, chips = half // PIECES, windows // 2
    parts = [pair[:, i * width : (i + 1) * width] for i in range(PIECES)]
    brought = [[lax.ppermute(part, "tm", [(i, i ^ 2) for i in range(windows)])] for part in parts]
    totals = [call(sum_kernel, [part.shape], (part, more))[0] for part, (more,) in zip(parts, brought)]
    carried = totals
    for hop in range(1, chips - 1):
        swap = [(i + 2 * a, i + 2 * b) for i in range(2) for a, b in ((hop, hop + 1), (hop + 1, hop))]
        moved = [lax.ppermute(part, "tm", swap) for part in carried]
        for earlier, more in zip(brought, moved):
            earlier.append(more)
        carried = moved if hop % 2 else [
            call(sum_kernel, [more.shape], (more, part))[0] for more, part in zip(moved, totals)
        ]
    (*brought[-1], c_all, d_all) = lax.optimization_barrier((*brought[-1], c_all, d_all))
    edge = (steps, half)
    send, start_own, to_onward, to_backward = call(
        functools.partial(prefix_kernel, PIECES, steps), [own.shape, own.shape, edge, edge],
        (own, pair, *(v for earlier in brought for v in earlier)))
    south_own, north_own = lax.ppermute(to_onward, "lat", onward), lax.ppermute(to_backward, "lat", backward)
    arrived = lax.ppermute(send, "tm", partner)
    c_all, coef_north, south_own = lax.optimization_barrier((c_all, coef_north, south_own))
    start_other, to_onward, to_backward = call(
        functools.partial(halo_kernel, steps), [own.shape, edge, edge], (other, arrived))
    south_other, north_other = lax.ppermute(to_onward, "lat", onward), lax.ppermute(to_backward, "lat", backward)

    work = 16 * steps * steps * columns
    even, odd = call(functools.partial(inner_kernel, steps), [field] * 2,
                     (paces, start_own, start_other, c_all, d_all), work=work)
    even, odd, final_south = call(
        functools.partial(south_kernel, steps), [field, field, (steps, columns)],
        (paces, south_own, south_other, c_all, d_all, even, odd), {5: 0, 6: 1}, work=work)
    previous_south = lax.ppermute(final_south, "tm", following)
    c_all, d_all = call(functools.partial(outer_coefficients_kernel, steps, steps + rows), [field] * 2,
                        (coef_north, c_all, d_all), {1: 0, 2: 1})
    _, _, final_north = call(
        functools.partial(north_kernel, steps), [field, field, (rows - steps, columns)],
        (paces, north_own, north_other, c_all, d_all, even, odd), {5: 0, 6: 1}, work=work)
    previous_north = lax.ppermute(final_north, "tm", following[:-1])
    results = write_results(0, previous_south, start_own, start_other, final_south, ())
    defect, final = write_results(steps, previous_north, start_own, start_other, final_north, results)
    return defect[None], final[None]


def solution(mesh):
    whole = P("tm", "lat", None)
    return jax.shard_map(
        on_device,
        mesh=mesh,
        in_specs=(whole, whole, whole, whole, P("tm", None)),
        out_specs=(whole, whole),
        check_vma=False,
    )
```

```python
import functools

import jax
import jax.numpy as jnp
from jax import lax
from jax.experimental import pallas as pl
from jax.experimental.pallas import tpu as pltpu
from jax.sharding import PartitionSpec as P

LANES = 128
PIECES = 2
VMEM = pl.BlockSpec(memory_space=pltpu.VMEM)


def call(kernel, out_shapes, args, aliases=None, work=0):
    return pl.pallas_call(
        kernel,
        out_shape=tuple(pltpu.VMEM(shape, jnp.float32) for shape in out_shapes),
        in_specs=[VMEM] * len(args),
        out_specs=(VMEM,) * len(out_shapes),
        input_output_aliases=aliases or {},
        cost_estimate=pl.CostEstimate(flops=work, bytes_accessed=0, transcendentals=0),
        compiler_params=pltpu.CompilerParams(vmem_limit_bytes=4 * 2**20),
    )(*(pltpu.with_memory_space_constraint(v, pltpu.VMEM) for v in args))


def has_band_before():
    return lax.axis_index("lat") > 0


def has_band_after():
    return lax.axis_index("lat") < lax.axis_size("lat") - 1


def columns_of(tile):
    return slice(tile * LANES, (tile + 1) * LANES)


def advance_rows(steps, rows_of, old_and_new, c_all, d_all, paces):
    tiles = c_all.shape[0]
    for step in range(1, steps + 1):
        first, stop = rows_of(step)
        if first >= stop:
            continue
        old, new = old_and_new if step % 2 else old_and_new[::-1]
        pace = paces[step - 1 : step, :]
        lane = lax.broadcasted_iota(jnp.int32, (stop - first, LANES), 1)
        for t in ((step + i) % tiles for i in range(tiles)):
            x = old[t, first:stop, :]
            east = pltpu.roll(jnp.where(lane == 0, old[(t + 1) % tiles, first:stop, :], x), LANES - 1, 1)
            west = pltpu.roll(jnp.where(lane == LANES - 1, old[(t - 1) % tiles, first:stop, :], x), 1, 1)
            ahead = old[t, first + 1 : stop + 1, :] - x
            behind = x - old[t, first - 1 : stop - 1, :]
            c = c_all[t, first:stop, :]
            d = d_all[t, first:stop, :]
            spread = ((east - x) + (west - x)) + (ahead - behind)
            new[t, first:stop, :] = x + (d * pace) * spread - c * jnp.where(c > 0, behind, ahead)


def sum_kernel(a, b, total):
    total[:, :] = a[:, :] + b[:, :]


def prefix_kernel(pieces, steps, own, pair, *refs):
    brought, (send, start_own, to_onward, to_backward) = refs[:-4], refs[-4:]
    hops = len(brought) // pieces
    width = own.shape[1] // pieces
    is_first, chip = lax.axis_index("tm") % 2 == 0, lax.axis_index("tm") // 2
    for piece in range(pieces):
        cols = slice(piece * width, (piece + 1) * width)
        before = jnp.where(chip % 2 == 1, brought[piece * hops][:, :], 0.0)
        for hop in range(1, hops):
            before = before + jnp.where(chip == hop + 1, brought[piece * hops + hop][:, :], 0.0)
        through_first = before + own[:, cols]
        send[:, cols] = jnp.where(is_first, through_first, before)
        start_own[:, cols] = jnp.where(is_first, through_first, before + pair[:, cols])
    to_onward[:, :] = start_own[own.shape[0] - steps :, :]
    to_backward[:, :] = start_own[:steps, :]


def halo_kernel(steps, other, arrived, start_other, to_onward, to_backward):
    start_other[:, :] = other[:, :] + arrived[:, :]
    to_onward[:, :] = start_other[other.shape[0] - steps :, :]
    to_backward[:, :] = start_other[:steps, :]


def pack_kernel(steps, courant, diffusion, onward, backward):
    rows = courant.shape[0]
    for at, field in ((0, courant), (steps, diffusion)):
        onward[at : at + steps, :] = field[rows - steps :, :]
        backward[at : at + steps, :] = field[:steps, :]


def inner_coefficients_kernel(steps, courant, diffusion, c_all, d_all):
    rows = courant.shape[0]
    for t in range(c_all.shape[0]):
        c_all[t, steps : steps + rows, :] = courant[:, columns_of(t)]
        d_all[t, steps : steps + rows, :] = diffusion[:, columns_of(t)]


def outer_coefficients_kernel(steps, at, side, c_in, d_in, c_all, d_all):
    del c_in, d_in
    exists = has_band_before() if at == 0 else has_band_after()
    for t in range(c_all.shape[0]):
        for which, whole in enumerate((c_all, d_all)):
            rows = side[which * steps : (which + 1) * steps, columns_of(t)]
            whole[t, at : at + steps, :] = jnp.where(exists, rows, 0.0)


def place_halves(own, other, rows, whole):
    half = whole.shape[0] // 2
    for t in range(half):
        for which, source in ((0, own), (1, other)):
            to = t + half * jnp.where(lax.axis_index("tm") % 2 == which, 0, 1)
            whole[to, rows, :] = source(columns_of(t))


def inner_kernel(steps, paces, own, other, c_all, d_all, even, odd):
    rows = own.shape[0]
    place_halves(lambda cols: own[:, cols], lambda cols: other[:, cols], slice(steps, steps + rows), even)
    advance_rows(steps, lambda n: (steps + n, steps + rows - n), (even, odd), c_all, d_all, paces)


def south_kernel(steps, paces, own, other, c_all, d_all, even_in, odd_in, even, odd, part):
    del even_in, odd_in
    exists = has_band_before()
    place_halves(lambda cols: jnp.where(exists, own[:, cols], 0.0),
                 lambda cols: jnp.where(exists, other[:, cols], 0.0), slice(0, steps), even)
    advance_rows(steps, lambda n: (n, steps + n), (even, odd), c_all, d_all, paces)
    last = odd if steps % 2 else even
    for t in range(last.shape[0]):
        part[:, columns_of(t)] = last[t, steps : 2 * steps, :]


def north_kernel(steps, paces, own, other, c_all, d_all, even_in, odd_in, even, odd, part):
    del even_in, odd_in
    exists = has_band_after()
    rows = c_all.shape[1] - 2 * steps
    place_halves(lambda cols: jnp.where(exists, own[:, cols], 0.0),
                 lambda cols: jnp.where(exists, other[:, cols], 0.0), slice(steps + rows, 2 * steps + rows), even)
    advance_rows(steps, lambda n: (steps + rows - n, 2 * steps + rows - n), (even, odd), c_all, d_all, paces)
    last = odd if steps % 2 else even
    for t in range(last.shape[0]):
        part[:, columns_of(t)] = last[t, 2 * steps : steps + rows, :]


def results_kernel(at, previous, own, other, final_part, *refs):
    defect, final, difference, sems = refs[-4:]
    count, half = previous.shape[0], own.shape[1]
    here = pl.ds(at, count)
    kept = pltpu.make_async_copy(final_part, final.at[here], sems.at[0])
    kept.start()
    is_first = lax.axis_index("tm") % 2 == 0
    follows = lax.axis_index("tm") > 0
    for low in range(0, half, LANES):
        a, b = own[at : at + count, low : low + LANES], other[at : at + count, low : low + LANES]
        for cols, start in (
            (slice(low, low + LANES), jnp.where(is_first, a, b)),
            (slice(half + low, half + low + LANES), jnp.where(is_first, b, a)),
        ):
            difference[:, cols] = start - jnp.where(follows, previous[:, cols], 0.0)
    made = pltpu.make_async_copy(difference, defect.at[here], sems.at[1])
    made.start()
    kept.wait()
    made.wait()


def write_results(at, previous, own, other, final_part, earlier):
    shape = (own.shape[0], 2 * own.shape[1])
    hbm = pl.BlockSpec(memory_space=pltpu.HBM)
    return pl.pallas_call(
        functools.partial(results_kernel, at),
        out_shape=(pltpu.HBM(shape, jnp.float32),) * 2,
        in_specs=[VMEM] * 4 + [hbm] * len(earlier),
        out_specs=(hbm, hbm),
        scratch_shapes=[pltpu.VMEM(previous.shape, jnp.float32), pltpu.SemaphoreType.DMA((2,))],
        input_output_aliases={4 + i: i for i in range(len(earlier))},
        compiler_params=pltpu.CompilerParams(vmem_limit_bytes=4 * 2**20),
    )(*(pltpu.with_memory_space_constraint(v, pltpu.VMEM) for v in (previous, own, other, final_part)), *earlier)


def on_device(control, scales, courant, diffusion, pacing):
    control, scales, courant, diffusion = (v[0] for v in (control, scales, courant, diffusion))
    steps = pacing.shape[1]
    rows, columns = control.shape
    half, tiles = columns // 2, columns // LANES
    windows, bands = lax.axis_size("tm"), lax.axis_size("lat")
    is_first = lax.axis_index("tm") % 2 == 0
    onward = [(i, (i + 1) % bands) for i in range(bands)]
    backward = [(j, i) for i, j in onward]
    partner = [(i, i ^ 1) for i in range(windows)]
    following = [(i, (i + 1) % windows) for i in range(windows)]
    paces = jnp.broadcast_to(pacing.reshape(steps, 1), (steps, LANES))

    increment = scales * control
    left, right = increment[:, :half], increment[:, half:]
    own = jnp.where(is_first, left, right)
    other = jnp.where(is_first, right, left)

    field = (tiles, rows + 2 * steps, LANES)
    to_onward, to_backward = call(functools.partial(pack_kernel, steps), [(2 * steps, columns)] * 2, (courant, diffusion))
    coef_south, coef_north = lax.ppermute(to_onward, "lat", onward), lax.ppermute(to_backward, "lat", backward)
    c_all, d_all = call(functools.partial(inner_coefficients_kernel, steps), [field] * 2, (courant, diffusion))
    c_all, d_all = call(functools.partial(outer_coefficients_kernel, steps, 0), [field] * 2,
                        (coef_south, c_all, d_all), {1: 0, 2: 1})

    (pair,) = call(sum_kernel, [own.shape], (own, lax.ppermute(other, "tm", partner)))
    width, chips = half // PIECES, windows // 2
    parts = [pair[:, i * width : (i + 1) * width] for i in range(PIECES)]
    brought = [[lax.ppermute(part, "tm", [(i, i ^ 2) for i in range(windows)])] for part in parts]
    totals = [call(sum_kernel, [part.shape], (part, more))[0] for part, (more,) in zip(parts, brought)]
    carried = totals
    for hop in range(1, chips - 1):
        swap = [(i + 2 * a, i + 2 * b) for i in range(2) for a, b in ((hop, hop + 1), (hop + 1, hop))]
        moved = [lax.ppermute(part, "tm", swap) for part in carried]
        for earlier, more in zip(brought, moved):
            earlier.append(more)
        carried = moved if hop % 2 else [
            call(sum_kernel, [more.shape], (more, part))[0] for more, part in zip(moved, totals)
        ]
    edge = (steps, half)
    send, start_own, to_onward, to_backward = call(
        functools.partial(prefix_kernel, PIECES, steps), [own.shape, own.shape, edge, edge],
        (own, pair, *(v for earlier in brought for v in earlier)))
    south_own, north_own = lax.ppermute(to_onward, "lat", onward), lax.ppermute(to_backward, "lat", backward)
    arrived = lax.ppermute(send, "tm", partner)
    arrived, c_all, d_all = lax.optimization_barrier((arrived, c_all, d_all))
    c_all, coef_north = lax.optimization_barrier((c_all, coef_north))
    start_other, to_onward, to_backward = call(
        functools.partial(halo_kernel, steps), [own.shape, edge, edge], (other, arrived))
    south_other, north_other = lax.ppermute(to_onward, "lat", onward), lax.ppermute(to_backward, "lat", backward)

    work = 16 * steps * steps * columns
    even, odd = call(functools.partial(inner_kernel, steps), [field] * 2,
                     (paces, start_own, start_other, c_all, d_all), work=work)
    even, odd, final_south = call(
        functools.partial(south_kernel, steps), [field, field, (steps, columns)],
        (paces, south_own, south_other, c_all, d_all, even, odd), {5: 0, 6: 1}, work=work)
    previous_south = lax.ppermute(final_south, "tm", following)
    c_all, d_all = call(functools.partial(outer_coefficients_kernel, steps, steps + rows), [field] * 2,
                        (coef_north, c_all, d_all), {1: 0, 2: 1})
    _, _, final_north = call(
        functools.partial(north_kernel, steps), [field, field, (rows - steps, columns)],
        (paces, north_own, north_other, c_all, d_all, even, odd), {5: 0, 6: 1}, work=work)
    previous_north = lax.ppermute(final_north, "tm", following[:-1])
    results = write_results(0, previous_south, start_own, start_other, final_south, ())
    defect, final = write_results(steps, previous_north, start_own, start_other, final_north, results)
    return defect[None], final[None]


def solution(mesh):
    whole = P("tm", "lat", None)
    return jax.shard_map(
        on_device,
        mesh=mesh,
        in_specs=(whole, whole, whole, whole, P("tm", None)),
        out_specs=(whole, whole),
        check_vma=False,
    )
```

```python
import functools

import jax
import jax.numpy as jnp
from jax import lax
from jax.experimental import pallas as pl
from jax.experimental.pallas import tpu as pltpu
from jax.sharding import PartitionSpec as P

LANES = 128
PIECES = 2
VMEM = pl.BlockSpec(memory_space=pltpu.VMEM)


def call(kernel, out_shapes, args, aliases=None, work=0):
    return pl.pallas_call(
        kernel,
        out_shape=tuple(pltpu.VMEM(shape, jnp.float32) for shape in out_shapes),
        in_specs=[VMEM] * len(args),
        out_specs=(VMEM,) * len(out_shapes),
        input_output_aliases=aliases or {},
        cost_estimate=pl.CostEstimate(flops=work, bytes_accessed=0, transcendentals=0),
        compiler_params=pltpu.CompilerParams(vmem_limit_bytes=4 * 2**20),
    )(*(pltpu.with_memory_space_constraint(v, pltpu.VMEM) for v in args))


def has_band_before():
    return lax.axis_index("lat") > 0


def has_band_after():
    return lax.axis_index("lat") < lax.axis_size("lat") - 1


def columns_of(tile):
    return slice(tile * LANES, (tile + 1) * LANES)


def advance_rows(steps, rows_of, old_and_new, c_all, d_all, paces):
    tiles = c_all.shape[0]
    for step in range(1, steps + 1):
        first, stop = rows_of(step)
        if first >= stop:
            continue
        old, new = old_and_new if step % 2 else old_and_new[::-1]
        pace = paces[step - 1 : step, :]
        lane = lax.broadcasted_iota(jnp.int32, (stop - first, LANES), 1)
        for t in ((step + i) % tiles for i in range(tiles)):
            x = old[t, first:stop, :]
            east = pltpu.roll(jnp.where(lane == 0, old[(t + 1) % tiles, first:stop, :], x), LANES - 1, 1)
            west = pltpu.roll(jnp.where(lane == LANES - 1, old[(t - 1) % tiles, first:stop, :], x), 1, 1)
            ahead = old[t, first + 1 : stop + 1, :] - x
            behind = x - old[t, first - 1 : stop - 1, :]
            c = c_all[t, first:stop, :]
            d = d_all[t, first:stop, :]
            spread = ((east - x) + (west - x)) + (ahead - behind)
            new[t, first:stop, :] = x + (d * pace) * spread - c * jnp.where(c > 0, behind, ahead)


def sum_kernel(a, b, total):
    total[:, :] = a[:, :] + b[:, :]


def prefix_kernel(pieces, steps, own, pair, *refs):
    brought, (send, start_own, to_onward, to_backward) = refs[:-4], refs[-4:]
    hops = len(brought) // pieces
    width = own.shape[1] // pieces
    is_first, chip = lax.axis_index("tm") % 2 == 0, lax.axis_index("tm") // 2
    for piece in range(pieces):
        cols = slice(piece * width, (piece + 1) * width)
        before = jnp.where(chip % 2 == 1, brought[piece * hops][:, :], 0.0)
        for hop in range(1, hops):
            before = before + jnp.where(chip == hop + 1, brought[piece * hops + hop][:, :], 0.0)
        through_first = before + own[:, cols]
        send[:, cols] = jnp.where(is_first, through_first, before)
        start_own[:, cols] = jnp.where(is_first, through_first, before + pair[:, cols])
    to_onward[:, :] = start_own[own.shape[0] - steps :, :]
    to_backward[:, :] = start_own[:steps, :]


def halo_kernel(steps, other, arrived, start_other, to_onward, to_backward):
    start_other[:, :] = other[:, :] + arrived[:, :]
    to_onward[:, :] = start_other[other.shape[0] - steps :, :]
    to_backward[:, :] = start_other[:steps, :]


def pack_kernel(steps, courant, diffusion, onward, backward):
    rows = courant.shape[0]
    for at, field in ((0, courant), (steps, diffusion)):
        onward[at : at + steps, :] = field[rows - steps :, :]
        backward[at : at + steps, :] = field[:steps, :]


def inner_coefficients_kernel(steps, courant, diffusion, c_all, d_all):
    rows = courant.shape[0]
    for t in range(c_all.shape[0]):
        c_all[t, steps : steps + rows, :] = courant[:, columns_of(t)]
        d_all[t, steps : steps + rows, :] = diffusion[:, columns_of(t)]


def outer_coefficients_kernel(steps, at, side, c_in, d_in, c_all, d_all):
    del c_in, d_in
    exists = has_band_before() if at == 0 else has_band_after()
    for t in range(c_all.shape[0]):
        for which, whole in enumerate((c_all, d_all)):
            rows = side[which * steps : (which + 1) * steps, columns_of(t)]
            whole[t, at : at + steps, :] = jnp.where(exists, rows, 0.0)


def place_halves(own, other, rows, whole):
    half = whole.shape[0] // 2
    for t in range(half):
        for which, source in ((0, own), (1, other)):
            to = t + half * jnp.where(lax.axis_index("tm") % 2 == which, 0, 1)
            whole[to, rows, :] = source(columns_of(t))


def inner_kernel(steps, paces, own, other, c_all, d_all, even, odd):
    rows = own.shape[0]
    place_halves(lambda cols: own[:, cols], lambda cols: other[:, cols], slice(steps, steps + rows), even)
    advance_rows(steps, lambda n: (steps + n, steps + rows - n), (even, odd), c_all, d_all, paces)


def south_kernel(steps, paces, own, other, c_all, d_all, even_in, odd_in, even, odd, part):
    del even_in, odd_in
    exists = has_band_before()
    place_halves(lambda cols: jnp.where(exists, own[:, cols], 0.0),
                 lambda cols: jnp.where(exists, other[:, cols], 0.0), slice(0, steps), even)
    advance_rows(steps, lambda n: (n, steps + n), (even, odd), c_all, d_all, paces)
    last = odd if steps % 2 else even
    for t in range(last.shape[0]):
        part[:, columns_of(t)] = last[t, steps : 2 * steps, :]


def north_kernel(steps, paces, own, other, c_all, d_all, even_in, odd_in, even, odd, part):
    del even_in, odd_in
    exists = has_band_after()
    rows = c_all.shape[1] - 2 * steps
    place_halves(lambda cols: jnp.where(exists, own[:, cols], 0.0),
                 lambda cols: jnp.where(exists, other[:, cols], 0.0), slice(steps + rows, 2 * steps + rows), even)
    advance_rows(steps, lambda n: (steps + rows - n, 2 * steps + rows - n), (even, odd), c_all, d_all, paces)
    last = odd if steps % 2 else even
    for t in range(last.shape[0]):
        part[:, columns_of(t)] = last[t, 2 * steps : steps + rows, :]


def results_kernel(at, copied, previous, own, other, *refs):
    parts, (difference, sems) = refs[:copied], refs[-2:]
    defect, *final = refs[copied:-2] if copied else refs[copied + 1 : -2]
    count, half = previous.shape[0], own.shape[1]
    copies, below = [], 0
    for part in parts:
        height = part.shape[0]
        copies.append(pltpu.make_async_copy(part, final[0].at[pl.ds(below, height)], sems.at[len(copies) + 1]))
        copies[-1].start()
        below += height
    is_first = lax.axis_index("tm") % 2 == 0
    follows = lax.axis_index("tm") > 0
    for low in range(0, half, LANES):
        a, b = own[at : at + count, low : low + LANES], other[at : at + count, low : low + LANES]
        for cols, start in (
            (slice(low, low + LANES), jnp.where(is_first, a, b)),
            (slice(half + low, half + low + LANES), jnp.where(is_first, b, a)),
        ):
            difference[:, cols] = start - jnp.where(follows, previous[:, cols], 0.0)
    copies.append(pltpu.make_async_copy(difference, defect.at[pl.ds(at, count)], sems.at[0]))
    copies[-1].start()
    for copy in copies:
        copy.wait()


def write_results(at, previous, own, other, parts=(), defect=None):
    shape = (own.shape[0], 2 * own.shape[1])
    hbm = pl.BlockSpec(memory_space=pltpu.HBM)
    earlier = () if defect is None else (defect,)
    results = 2 if parts else 1
    in_vmem = (previous, own, other, *parts)
    return pl.pallas_call(
        functools.partial(results_kernel, at, len(parts)),
        out_shape=(pltpu.HBM(shape, jnp.float32),) * results,
        in_specs=[VMEM] * len(in_vmem) + [hbm] * len(earlier),
        out_specs=(hbm,) * results,
        scratch_shapes=[pltpu.VMEM(previous.shape, jnp.float32), pltpu.SemaphoreType.DMA((1 + len(parts),))],
        input_output_aliases={len(in_vmem): 0} if earlier else {},
        compiler_params=pltpu.CompilerParams(vmem_limit_bytes=4 * 2**20),
    )(*(pltpu.with_memory_space_constraint(v, pltpu.VMEM) for v in in_vmem), *earlier)


def on_device(control, scales, courant, diffusion, pacing):
    control, scales, courant, diffusion = (v[0] for v in (control, scales, courant, diffusion))
    steps = pacing.shape[1]
    rows, columns = control.shape
    half, tiles = columns // 2, columns // LANES
    windows, bands = lax.axis_size("tm"), lax.axis_size("lat")
    is_first = lax.axis_index("tm") % 2 == 0
    onward = [(i, (i + 1) % bands) for i in range(bands)]
    backward = [(j, i) for i, j in onward]
    partner = [(i, i ^ 1) for i in range(windows)]
    following = [(i, (i + 1) % windows) for i in range(windows)]
    paces = jnp.broadcast_to(pacing.reshape(steps, 1), (steps, LANES))

    increment = scales * control
    left, right = increment[:, :half], increment[:, half:]
    own = jnp.where(is_first, left, right)
    other = jnp.where(is_first, right, left)

    field = (tiles, rows + 2 * steps, LANES)
    to_onward, to_backward = call(functools.partial(pack_kernel, steps), [(2 * steps, columns)] * 2, (courant, diffusion))
    coef_south, coef_north = lax.ppermute(to_onward, "lat", onward), lax.ppermute(to_backward, "lat", backward)
    c_all, d_all = call(functools.partial(inner_coefficients_kernel, steps), [field] * 2, (courant, diffusion))
    c_all, d_all = call(functools.partial(outer_coefficients_kernel, steps, 0), [field] * 2,
                        (coef_south, c_all, d_all), {1: 0, 2: 1})

    (pair,) = call(sum_kernel, [own.shape], (own, lax.ppermute(other, "tm", partner)))
    width, chips = half // PIECES, windows // 2
    parts = [pair[:, i * width : (i + 1) * width] for i in range(PIECES)]
    brought = [[lax.ppermute(part, "tm", [(i, i ^ 2) for i in range(windows)])] for part in parts]
    totals = [call(sum_kernel, [part.shape], (part, more))[0] for part, (more,) in zip(parts, brought)]
    carried = totals
    for hop in range(1, chips - 1):
        step = [(2 * hop + i, 2 * hop + 2 + i) for i in range(2)]
        moved = [lax.ppermute(part, "tm", step) for part in carried]
        for earlier, more in zip(brought, moved):
            earlier.append(more)
        carried = moved if hop % 2 else [
            call(sum_kernel, [more.shape], (more, part))[0] for more, part in zip(moved, totals)
        ]
    edge = (steps, half)
    send, start_own, to_onward, to_backward = call(
        functools.partial(prefix_kernel, PIECES, steps), [own.shape, own.shape, edge, edge],
        (own, pair, *(v for earlier in brought for v in earlier)))
    south_own, north_own = lax.ppermute(to_onward, "lat", onward), lax.ppermute(to_backward, "lat", backward)
    send, c_all, d_all = lax.optimization_barrier((send, c_all, d_all))
    arrived = lax.ppermute(send, "tm", partner)
    c_all, coef_north = lax.optimization_barrier((c_all, coef_north))
    start_other, to_onward, to_backward = call(
        functools.partial(halo_kernel, steps), [own.shape, edge, edge], (other, arrived))
    south_other, north_other = lax.ppermute(to_onward, "lat", onward), lax.ppermute(to_backward, "lat", backward)

    work = 16 * steps * steps * columns
    even, odd = call(functools.partial(inner_kernel, steps), [field] * 2,
                     (paces, start_own, start_other, c_all, d_all), work=work)
    even, odd, final_south = call(
        functools.partial(south_kernel, steps), [field, field, (steps, columns)],
        (paces, south_own, south_other, c_all, d_all, even, odd), {5: 0, 6: 1}, work=work)
    previous_south = lax.ppermute(final_south, "tm", following)
    c_all, d_all = call(functools.partial(outer_coefficients_kernel, steps, steps + rows), [field] * 2,
                        (coef_north, c_all, d_all), {1: 0, 2: 1})
    _, _, final_north = call(
        functools.partial(north_kernel, steps), [field, field, (rows - steps, columns)],
        (paces, north_own, north_other, c_all, d_all, even, odd), {5: 0, 6: 1}, work=work)
    previous_north = lax.ppermute(final_north, "tm", following[:-1])
    defect, final = write_results(0, previous_south, start_own, start_other, (final_south, final_north))
    (defect,) = write_results(steps, previous_north, start_own, start_other, defect=defect)
    return defect[None], final[None]


def solution(mesh):
    whole = P("tm", "lat", None)
    return jax.shard_map(
        on_device,
        mesh=mesh,
        in_specs=(whole, whole, whole, whole, P("tm", None)),
        out_specs=(whole, whole),
        check_vma=False,
    )
```

```python
import functools

import jax
import jax.numpy as jnp
from jax import lax
from jax.experimental import pallas as pl
from jax.experimental.pallas import tpu as pltpu
from jax.sharding import PartitionSpec as P

LANES = 128
PIECES = 2
VMEM = pl.BlockSpec(memory_space=pltpu.VMEM)


def call(kernel, out_shapes, args, aliases=None, work=0):
    return pl.pallas_call(
        kernel,
        out_shape=tuple(pltpu.VMEM(shape, jnp.float32) for shape in out_shapes),
        in_specs=[VMEM] * len(args),
        out_specs=(VMEM,) * len(out_shapes),
        input_output_aliases=aliases or {},
        cost_estimate=pl.CostEstimate(flops=work, bytes_accessed=0, transcendentals=0),
        compiler_params=pltpu.CompilerParams(vmem_limit_bytes=4 * 2**20),
    )(*(pltpu.with_memory_space_constraint(v, pltpu.VMEM) for v in args))


def has_band_before():
    return lax.axis_index("lat") > 0


def has_band_after():
    return lax.axis_index("lat") < lax.axis_size("lat") - 1


def columns_of(tile):
    return slice(tile * LANES, (tile + 1) * LANES)


def advance_rows(steps, rows_of, old_and_new, c_all, d_all, paces):
    tiles = c_all.shape[0]
    for step in range(1, steps + 1):
        first, stop = rows_of(step)
        if first >= stop:
            continue
        old, new = old_and_new if step % 2 else old_and_new[::-1]
        pace = paces[step - 1 : step, :]
        lane = lax.broadcasted_iota(jnp.int32, (stop - first, LANES), 1)

        def eastward(t):
            x = old[t, first:stop, :]
            return x, pltpu.roll(jnp.where(lane == 0, old[(t + 1) % tiles, first:stop, :], x), LANES - 1, 1) - x

        _, west_of = eastward((step - 1) % tiles)
        for t in ((step + i) % tiles for i in range(tiles)):
            x, east = eastward(t)
            west = pltpu.roll(jnp.where(lane == LANES - 1, west_of, east), 1, 1)
            west_of = east
            ahead = old[t, first + 1 : stop + 1, :] - x
            behind = x - old[t, first - 1 : stop - 1, :]
            c = c_all[t, first:stop, :]
            d = d_all[t, first:stop, :]
            spread = (east - west) + (ahead - behind)
            new[t, first:stop, :] = x + (d * pace) * spread - c * jnp.where(c > 0, behind, ahead)


def sum_kernel(a, b, total):
    total[:, :] = a[:, :] + b[:, :]


def prefix_kernel(pieces, steps, own, pair, *refs):
    brought, (send, start_own, to_onward, to_backward) = refs[:-4], refs[-4:]
    hops = len(brought) // pieces
    width = own.shape[1] // pieces
    is_first, chip = lax.axis_index("tm") % 2 == 0, lax.axis_index("tm") // 2
    for piece in range(pieces):
        cols = slice(piece * width, (piece + 1) * width)
        before = jnp.where(chip % 2 == 1, brought[piece * hops][:, :], 0.0)
        for hop in range(1, hops):
            before = before + jnp.where(chip == hop + 1, brought[piece * hops + hop][:, :], 0.0)
        through_first = before + own[:, cols]
        send[:, cols] = jnp.where(is_first, through_first, before)
        start_own[:, cols] = jnp.where(is_first, through_first, before + pair[:, cols])
    to_onward[:, :] = start_own[own.shape[0] - steps :, :]
    to_backward[:, :] = start_own[:steps, :]


def halo_kernel(steps, other, arrived, start_other, to_onward, to_backward):
    start_other[:, :] = other[:, :] + arrived[:, :]
    to_onward[:, :] = start_other[other.shape[0] - steps :, :]
    to_backward[:, :] = start_other[:steps, :]


def pack_kernel(steps, courant, diffusion, onward, backward):
    rows = courant.shape[0]
    for at, field in ((0, courant), (steps, diffusion)):
        onward[at : at + steps, :] = field[rows - steps :, :]
        backward[at : at + steps, :] = field[:steps, :]


def inner_coefficients_kernel(steps, courant, diffusion, c_all, d_all):
    rows = courant.shape[0]
    for t in range(c_all.shape[0]):
        c_all[t, steps : steps + rows, :] = courant[:, columns_of(t)]
        d_all[t, steps : steps + rows, :] = diffusion[:, columns_of(t)]


def outer_coefficients_kernel(steps, at, side, c_in, d_in, c_all, d_all):
    del c_in, d_in
    exists = has_band_before() if at == 0 else has_band_after()
    for t in range(c_all.shape[0]):
        for which, whole in enumerate((c_all, d_all)):
            rows = side[which * steps : (which + 1) * steps, columns_of(t)]
            whole[t, at : at + steps, :] = jnp.where(exists, rows, 0.0)


def place_halves(own, other, rows, whole):
    half = whole.shape[0] // 2
    for t in range(half):
        for which, source in ((0, own), (1, other)):
            to = t + half * jnp.where(lax.axis_index("tm") % 2 == which, 0, 1)
            whole[to, rows, :] = source(columns_of(t))


def inner_kernel(steps, paces, own, other, c_all, d_all, even, odd):
    rows = own.shape[0]
    place_halves(lambda cols: own[:, cols], lambda cols: other[:, cols], slice(steps, steps + rows), even)
    advance_rows(steps, lambda n: (steps + n, steps + rows - n), (even, odd), c_all, d_all, paces)


def south_kernel(steps, paces, own, other, c_all, d_all, even_in, odd_in, even, odd, part):
    del even_in, odd_in
    exists = has_band_before()
    place_halves(lambda cols: jnp.where(exists, own[:, cols], 0.0),
                 lambda cols: jnp.where(exists, other[:, cols], 0.0), slice(0, steps), even)
    advance_rows(steps, lambda n: (n, steps + n), (even, odd), c_all, d_all, paces)
    last = odd if steps % 2 else even
    for t in range(last.shape[0]):
        part[:, columns_of(t)] = last[t, steps : 2 * steps, :]


def north_kernel(steps, paces, own, other, c_all, d_all, even_in, odd_in, even, odd, part):
    del even_in, odd_in
    exists = has_band_after()
    rows = c_all.shape[1] - 2 * steps
    place_halves(lambda cols: jnp.where(exists, own[:, cols], 0.0),
                 lambda cols: jnp.where(exists, other[:, cols], 0.0), slice(steps + rows, 2 * steps + rows), even)
    advance_rows(steps, lambda n: (steps + rows - n, 2 * steps + rows - n), (even, odd), c_all, d_all, paces)
    last = odd if steps % 2 else even
    for t in range(last.shape[0]):
        part[:, columns_of(t)] = last[t, 2 * steps : steps + rows, :]


def results_kernel(at, copied, previous, own, other, *refs):
    parts, (difference, sems) = refs[:copied], refs[-2:]
    defect, *final = refs[copied:-2] if copied else refs[copied + 1 : -2]
    count, half = previous.shape[0], own.shape[1]
    copies, below = [], 0
    for part in parts:
        height = part.shape[0]
        copies.append(pltpu.make_async_copy(part, final[0].at[pl.ds(below, height)], sems.at[len(copies) + 1]))
        copies[-1].start()
        below += height
    is_first = lax.axis_index("tm") % 2 == 0
    follows = lax.axis_index("tm") > 0
    for low in range(0, half, LANES):
        a, b = own[at : at + count, low : low + LANES], other[at : at + count, low : low + LANES]
        for cols, start in (
            (slice(low, low + LANES), jnp.where(is_first, a, b)),
            (slice(half + low, half + low + LANES), jnp.where(is_first, b, a)),
        ):
            difference[:, cols] = start - jnp.where(follows, previous[:, cols], 0.0)
    copies.append(pltpu.make_async_copy(difference, defect.at[pl.ds(at, count)], sems.at[0]))
    copies[-1].start()
    for copy in copies:
        copy.wait()


def write_results(at, previous, own, other, parts=(), defect=None):
    shape = (own.shape[0], 2 * own.shape[1])
    hbm = pl.BlockSpec(memory_space=pltpu.HBM)
    earlier = () if defect is None else (defect,)
    results = 2 if parts else 1
    in_vmem = (previous, own, other, *parts)
    return pl.pallas_call(
        functools.partial(results_kernel, at, len(parts)),
        out_shape=(pltpu.HBM(shape, jnp.float32),) * results,
        in_specs=[VMEM] * len(in_vmem) + [hbm] * len(earlier),
        out_specs=(hbm,) * results,
        scratch_shapes=[pltpu.VMEM(previous.shape, jnp.float32), pltpu.SemaphoreType.DMA((1 + len(parts),))],
        input_output_aliases={len(in_vmem): 0} if earlier else {},
        compiler_params=pltpu.CompilerParams(vmem_limit_bytes=4 * 2**20),
    )(*(pltpu.with_memory_space_constraint(v, pltpu.VMEM) for v in in_vmem), *earlier)


def on_device(control, scales, courant, diffusion, pacing):
    control, scales, courant, diffusion = (v[0] for v in (control, scales, courant, diffusion))
    steps = pacing.shape[1]
    rows, columns = control.shape
    half, tiles = columns // 2, columns // LANES
    windows, bands = lax.axis_size("tm"), lax.axis_size("lat")
    is_first = lax.axis_index("tm") % 2 == 0
    onward = [(i, (i + 1) % bands) for i in range(bands)]
    backward = [(j, i) for i, j in onward]
    partner = [(i, i ^ 1) for i in range(windows)]
    following = [(i, (i + 1) % windows) for i in range(windows)]
    paces = jnp.broadcast_to(pacing.reshape(steps, 1), (steps, LANES))

    increment = scales * control
    left, right = increment[:, :half], increment[:, half:]
    own = jnp.where(is_first, left, right)
    other = jnp.where(is_first, right, left)

    field = (tiles, rows + 2 * steps, LANES)
    to_onward, to_backward = call(functools.partial(pack_kernel, steps), [(2 * steps, columns)] * 2, (courant, diffusion))
    coef_south, coef_north = lax.ppermute(to_onward, "lat", onward), lax.ppermute(to_backward, "lat", backward)
    c_all, d_all = call(functools.partial(inner_coefficients_kernel, steps), [field] * 2, (courant, diffusion))
    c_all, d_all = call(functools.partial(outer_coefficients_kernel, steps, 0), [field] * 2,
                        (coef_south, c_all, d_all), {1: 0, 2: 1})

    (pair,) = call(sum_kernel, [own.shape], (own, lax.ppermute(other, "tm", partner)))
    width, chips = half // PIECES, windows // 2
    parts = [pair[:, i * width : (i + 1) * width] for i in range(PIECES)]
    brought = [[lax.ppermute(part, "tm", [(i, i ^ 2) for i in range(windows)])] for part in parts]
    totals = [call(sum_kernel, [part.shape], (part, more))[0] for part, (more,) in zip(parts, brought)]
    carried = totals
    for hop in range(1, chips - 1):
        step = [(2 * hop + i, 2 * hop + 2 + i) for i in range(2)]
        moved = [lax.ppermute(part, "tm", step) for part in carried]
        for earlier, more in zip(brought, moved):
            earlier.append(more)
        carried = moved if hop % 2 else [
            call(sum_kernel, [more.shape], (more, part))[0] for more, part in zip(moved, totals)
        ]
    edge = (steps, half)
    send, start_own, to_onward, to_backward = call(
        functools.partial(prefix_kernel, PIECES, steps), [own.shape, own.shape, edge, edge],
        (own, pair, *(v for earlier in brought for v in earlier)))
    south_own, north_own = lax.ppermute(to_onward, "lat", onward), lax.ppermute(to_backward, "lat", backward)
    send, c_all, d_all = lax.optimization_barrier((send, c_all, d_all))
    arrived = lax.ppermute(send, "tm", partner)
    c_all, coef_north = lax.optimization_barrier((c_all, coef_north))
    start_other, to_onward, to_backward = call(
        functools.partial(halo_kernel, steps), [own.shape, edge, edge], (other, arrived))
    south_other, north_other = lax.ppermute(to_onward, "lat", onward), lax.ppermute(to_backward, "lat", backward)

    work = 16 * steps * steps * columns
    even, odd = call(functools.partial(inner_kernel, steps), [field] * 2,
                     (paces, start_own, start_other, c_all, d_all), work=work)
    even, odd, final_south = call(
        functools.partial(south_kernel, steps), [field, field, (steps, columns)],
        (paces, south_own, south_other, c_all, d_all, even, odd), {5: 0, 6: 1}, work=work)
    previous_south = lax.ppermute(final_south, "tm", following)
    c_all, d_all = call(functools.partial(outer_coefficients_kernel, steps, steps + rows), [field] * 2,
                        (coef_north, c_all, d_all), {1: 0, 2: 1})
    _, _, final_north = call(
        functools.partial(north_kernel, steps), [field, field, (rows - steps, columns)],
        (paces, north_own, north_other, c_all, d_all, even, odd), {5: 0, 6: 1}, work=work)
    previous_north = lax.ppermute(final_north, "tm", following[:-1])
    defect, final = write_results(0, previous_south, start_own, start_other, (final_south, final_north))
    (defect,) = write_results(steps, previous_north, start_own, start_other, defect=defect)
    return defect[None], final[None]


def solution(mesh):
    whole = P("tm", "lat", None)
    return jax.shard_map(
        on_device,
        mesh=mesh,
        in_specs=(whole, whole, whole, whole, P("tm", None)),
        out_specs=(whole, whole),
        check_vma=False,
    )
```
